32 devices in a mesh: ctx: 16 (over z, x, core), head: 2 (over y).
Axes of the slice: x: 2, y: 2, z: 4, core: 2. Of those that a mesh axis runs over, the one named last changes fastest.
Arguments:
- query: bfloat16 [4096, 32, 128], P('ctx', 'head'), may hold values from -160 to 160
- key: bfloat16 [4096, 8, 128], P('ctx', 'head'), may hold values from -8 to 8
- value: bfloat16 [4096, 8, 128], P('ctx', 'head'), may hold values from -6 to 6
- d_mixed: bfloat16 [4096, 4096], P('ctx', 'head'), may hold values from -6 to 6
- out_weight: bfloat16 [4096, 4096], P('head'), may hold values from -1 to 1
- block_keys: int32 [32, 20], P('ctx'), may hold values from 0 to 31, as said below
- scope_ids: int32 [4096], P('ctx'), may hold values from 0 to 15
Outputs:
- grad_query: bfloat16 [4096, 32, 128], P('ctx', 'head')
- grad_key: bfloat16 [4096, 8, 128], P('ctx', 'head')
- grad_value: bfloat16 [4096, 8, 128], P('ctx', 'head')
The draws below stay inside these ranges and needn't reach their ends.
Inputs may be any that keep to these rules, and one draw needn't show every extreme that they name: `block_keys`: row b names 20 distinct key blocks, block b itself among them.
All inputs are finite; a program needn't handle non-finite values.
Results may differ from the reference program's by a relative error of at most 0.0059.
Values may be sent and summed in bfloat16 or wider, within the bound.
A program may use at most 192 MiB of HBM per device.

```python
import math
import jax
import jax.numpy as jnp
from jax import lax

HQ = 32
KVH = 8
DH = 128
D = 4096
BLK = 128
NSCOPE = 16
S = 4096
SCOPE_BLOCKS = 32
KSLOT = 20


def draw_pair(key):
    base = jax.random.fold_in(key, 11)
    first, second = jax.random.split(base, 2)
    keys = jnp.clip(jax.random.normal(first, (S, KVH, DH), jnp.float32), -6.0, 6.0)
    queries = jnp.clip(jax.random.normal(second, (S, HQ, DH), jnp.float32), -6.0, 6.0)
    return (queries, keys)


def draw_query(key, part):
    return draw_pair(key)[0].astype(jnp.bfloat16)


def draw_key(key, part):
    return draw_pair(key)[1].astype(jnp.bfloat16)


def draw_block_keys(key, part):
    first, second = jax.random.split(jax.random.fold_in(key, 5), 2)
    random_jitter = jax.random.randint(first, (SCOPE_BLOCKS, SCOPE_BLOCKS), 0, 4096)
    central_nodes = jax.random.randint(second, (SCOPE_BLOCKS,), 0, 4)
    rows_at = jnp.arange(SCOPE_BLOCKS)[:, None]
    column_positions = jnp.arange(SCOPE_BLOCKS)[None, :]
    stride_distance = jnp.abs(rows_at - column_positions)
    extra_reward = jnp.maximum(0, 6 - stride_distance) * 1024 + central_nodes[None, :] * 1500 + jnp.where(stride_distance == 0, 1 << 20, 0)
    score_entry = (random_jitter + extra_reward) * SCOPE_BLOCKS + column_positions
    return lax.top_k(score_entry, KSLOT)[1].astype(jnp.int32)


def place_ends(entries, stream_key, low, high):
    spot = [jax.random.randint(jax.random.fold_in(stream_key, axis), (), 0, length) for axis, length in enumerate(entries.shape)]
    main_axis = entries.shape.index(max(entries.shape))
    beside = spot[:main_axis] + [(spot[main_axis] + 1) % entries.shape[main_axis]] + spot[main_axis + 1:]
    return entries.at[tuple(spot)].set(low).at[tuple(beside)].set(high)


def steps_of(key, extent, cuts, low, top_value):
    gain, own = 1.0, jax.random.fold_in(key, 6)
    for position, blocks in cuts:
        draws = jnp.exp(jax.random.uniform(jax.random.fold_in(own, position), (blocks,), jnp.float32, low / len(cuts), top_value / len(cuts)))
        gain = gain * jnp.repeat(draws, extent[position] // blocks).reshape([-1 if axis == position else 1 for axis in range(len(extent))])
    return gain


def bell_draw(key, extent, spread, bound, shards=(), held_as=jnp.bfloat16):
    values = jax.random.normal(key, extent, jnp.float32) * spread
    if len(shards) > 0:
        values = steps_of(key, extent, shards, -0.22, 0.18) * values
    return jnp.clip(values, min=-bound, max=bound).astype(held_as)


def setup_inputs(seed: int = 0) -> dict:
    splits = jax.random.split(jax.random.key(seed), 8)
    return {
        "query": draw_query(jax.random.fold_in(splits[7], 71), 0),
        "key": draw_key(jax.random.fold_in(splits[7], 71), 0),
        "value": bell_draw(splits[2], (S, KVH, DH), 1.0, 6.0, ((0, 16), (1, 2))),
        "d_mixed": bell_draw(splits[3], (S, D), 1.0, 6.0, ((0, 16), (1, 2))),
        "out_weight": bell_draw(splits[4], (HQ * DH, D), (max(D // 100, 1)) ** -0.5, 1.0, ((0, 2),)),
        "block_keys": draw_block_keys(jax.random.fold_in(splits[7], 71), 0),
        "scope_ids": place_ends(jax.random.randint(splits[6], (S,), 0, NSCOPE), jax.random.fold_in(splits[6], 1), 0, NSCOPE - 1).astype(jnp.int32),
    }


def reference(query, key, value, d_mixed, out_weight, block_keys, scope_ids):
    group = HQ // KVH
    scale = 1.0 / math.sqrt(DH)
    d_out = jnp.dot(d_mixed, out_weight.T, preferred_element_type=jnp.float32).astype(jnp.bfloat16)
    q_blocks = query.reshape(SCOPE_BLOCKS, BLK, KVH, group, DH)
    do_blocks = d_out.reshape(SCOPE_BLOCKS, BLK, KVH, group, DH)
    k_blocks = key.reshape(SCOPE_BLOCKS, BLK, KVH, DH)
    v_blocks = value.reshape(SCOPE_BLOCKS, BLK, KVH, DH)
    s_blocks = scope_ids.reshape(SCOPE_BLOCKS, BLK)

    def one_block(carry, inputs):
        grad_k, grad_v = carry
        q_here, do_here, scope_here, listed = inputs
        listed = listed.astype(jnp.int32)
        keys_near = k_blocks[listed].reshape(KSLOT * BLK, KVH, DH).astype(jnp.float32)
        vals_near = v_blocks[listed].reshape(KSLOT * BLK, KVH, DH).astype(jnp.float32)
        scope_near = s_blocks[listed].reshape(KSLOT * BLK)
        visible = (scope_near[None, :] == scope_here[:, None]) | (scope_near[None, :] == 0)
        q_float = q_here.astype(jnp.float32)
        do_float = do_here.astype(jnp.float32)
        scores = jnp.einsum('ignd,jgd->gnij', q_float, keys_near) * scale
        masked = jnp.where(visible, scores, -jnp.inf)
        lse = jax.nn.logsumexp(masked, axis=-1)
        probs = jnp.where(visible, jnp.exp(scores - lse[..., None]), 0.0)
        attn_out = jnp.einsum('gnij,jgd->ignd', probs, vals_near, precision=lax.Precision.HIGHEST)
        delta = jnp.transpose(lax.optimization_barrier(jnp.sum(do_float * attn_out, axis=-1)), (1, 2, 0))
        rounded = lax.optimization_barrier(probs.astype(jnp.bfloat16)).astype(jnp.float32)
        part_v = jnp.einsum('gnij,ignd->jgd', rounded, do_float)
        dprobs = jnp.einsum('ignd,jgd->gnij', do_float, vals_near)
        dscores = probs * (dprobs - delta[..., None]) * scale
        dscores = lax.optimization_barrier(dscores.astype(jnp.bfloat16)).astype(jnp.float32)
        grad_q = jnp.einsum('gnij,jgd->ignd', dscores, keys_near).astype(jnp.bfloat16)
        part_k = jnp.einsum('gnij,ignd->jgd', dscores, q_float)
        grad_k = grad_k.at[listed].add(part_k.reshape(KSLOT, BLK, KVH, DH))
        grad_v = grad_v.at[listed].add(part_v.reshape(KSLOT, BLK, KVH, DH))
        return ((grad_k, grad_v), grad_q)
    zeros = jnp.zeros((SCOPE_BLOCKS, BLK, KVH, DH), jnp.float32)
    (grad_k, grad_v), grad_q = lax.scan(one_block, (zeros, zeros), (q_blocks, do_blocks, s_blocks, block_keys))
    return (grad_q.reshape(S, HQ, DH), grad_k.reshape(S, KVH, DH).astype(jnp.bfloat16), grad_v.reshape(S, KVH, DH).astype(jnp.bfloat16))
```

```python
import functools
import math

import jax
import jax.numpy as jnp
from jax import lax
from jax.experimental import pallas as pl
from jax.experimental.pallas import tpu as pltpu
from jax.sharding import PartitionSpec as P

BLK = 128
PAD = 16
F32 = jnp.float32
BF16 = jnp.bfloat16
NT = (((1,), (1,)), ((), ()))
TN = (((0,), (0,)), ((), ()))


def attend_kernel(
    devices, tokens, kv, group, slots, listed, q_ref, do_ref, kv_ref, own_ref, gq_ref, part_ref,
    acc, s_scr, dp_scr, scope_scr, qg, dg, gq_acc,
):
    blocks = tokens // BLK
    width = BLK
    wide = group * BLK
    cut = next(c for c in (4, 2, 1) if slots % c == 0)
    chunk = cut * BLK
    scale = 1.0 / math.sqrt(width)
    log2e = scale * math.log2(math.e)

    def fill(d, _):
        tile = kv_ref[pl.ds(pl.multiple_of(d * (tokens + PAD) + tokens, PAD), PAD), 0:tokens]
        for b in range(blocks):
            row = tile[0:1, b * BLK : (b + 1) * BLK].astype(F32)
            at = pl.multiple_of((d * blocks + b) * BLK, BLK)
            scope_scr[pl.ds(at, BLK), :] = jnp.broadcast_to(row, (BLK, BLK)).T
        return 0

    lax.fori_loop(0, devices, fill, 0)

    def rows_of(j):
        d = j // blocks
        return pl.ds(pl.multiple_of(d * (tokens + PAD) + (j - d * blocks) * BLK, PAD), BLK)

    def head_loop(g, _):
        k_cols = pl.ds(pl.multiple_of(g * width, width), width)
        v_cols = pl.ds(pl.multiple_of((kv + g) * width, width), width)
        acc[...] = jnp.zeros_like(acc)

        def row_loop(r, _):
            q_rows = pl.ds(pl.multiple_of(r * BLK, BLK), BLK)

            def head_cols(n):
                return pl.ds(pl.multiple_of((g * group + n) * width, width), width)

            for n in range(group):
                qg[n * BLK : (n + 1) * BLK, :] = q_ref[q_rows, head_cols(n)]
                dg[n * BLK : (n + 1) * BLK, :] = do_ref[q_rows, head_cols(n)]
            own = own_ref[pl.ds(r, 1), :]

            def listed_rows(c):
                return [listed[r, c * cut + u] for u in range(cut)]

            def near(c, cols):
                return jnp.concatenate([kv_ref[rows_of(j), cols] for j in listed_rows(c)], axis=0)

            def here(c):
                return pl.ds(pl.multiple_of(c * chunk, chunk), chunk)

            def first(c, high):
                s = lax.dot_general(near(c, k_cols), qg[...], NT, preferred_element_type=F32)
                bias = []
                for j in listed_rows(c):
                    sk = scope_scr[pl.ds(pl.multiple_of(j * BLK, BLK), BLK), :]
                    b = jnp.where((sk == own) | (sk == 0.0), 0.0, -1e30)
                    bias.append(jnp.concatenate([b] * group, axis=1))
                s = s + jnp.concatenate(bias, axis=0)
                s_scr[here(c), :] = s
                return jnp.maximum(high, jnp.max(s, axis=0, keepdims=True))

            high = lax.fori_loop(0, slots // cut, first, jnp.full((1, wide), -1e30, F32))

            def second(c, carry):
                total, delta = carry
                p = jnp.exp2((s_scr[here(c), :] - high) * log2e)
                dp = lax.dot_general(near(c, v_cols), dg[...], NT, preferred_element_type=F32)
                s_scr[here(c), :] = p
                dp_scr[here(c), :] = dp
                return (
                    total + jnp.sum(p, axis=0, keepdims=True),
                    delta + jnp.sum(p * dp, axis=0, keepdims=True),
                )

            zero = jnp.zeros((1, wide), F32)
            total, delta = lax.fori_loop(0, slots // cut, second, (zero, zero))
            inverse = 1.0 / total
            delta = delta * inverse
            gq_acc[...] = jnp.zeros_like(gq_acc)

            def third(c, _):
                pn = s_scr[here(c), :] * inverse
                ds = (pn * ((dp_scr[here(c), :] - delta) * scale)).astype(BF16)
                gv = jnp.dot(pn.astype(BF16), dg[...], preferred_element_type=F32)
                gk = jnp.dot(ds, qg[...], preferred_element_type=F32)
                gq_acc[...] += lax.dot_general(near(c, k_cols), ds, TN, preferred_element_type=F32)
                for u, j in enumerate(listed_rows(c)):
                    at = pl.ds(pl.multiple_of(j * BLK, BLK), BLK)
                    acc[at, 0:width] += gk[u * BLK : (u + 1) * BLK, :]
                    acc[at, width : 2 * width] += gv[u * BLK : (u + 1) * BLK, :]
                return 0

            lax.fori_loop(0, slots // cut, third, 0)
            for n in range(group):
                gq_ref[q_rows, head_cols(n)] = gq_acc[:, n * BLK : (n + 1) * BLK].T.astype(BF16)
            return 0

        lax.fori_loop(0, blocks, row_loop, 0)
        part_ref[:, k_cols] = acc[:, 0:width].astype(BF16)
        part_ref[:, v_cols] = acc[:, width : 2 * width].astype(BF16)
        return 0

    lax.fori_loop(0, kv, head_loop, 0)


def attend(listed, q, do, kv_all, own, devices, kv):
    tokens = q.shape[0]
    group = q.shape[1] // BLK // kv
    slots = listed.shape[1]
    total = devices * tokens
    wide = group * BLK
    vmem = pl.BlockSpec(memory_space=pltpu.VMEM)
    return pl.pallas_call(
        functools.partial(attend_kernel, devices, tokens, kv, group, slots),
        out_shape=(
            jax.ShapeDtypeStruct(q.shape, BF16),
            jax.ShapeDtypeStruct((total, 2 * kv * BLK), BF16),
        ),
        in_specs=[pl.BlockSpec(memory_space=pltpu.SMEM)] + [vmem] * 4,
        out_specs=(vmem, vmem),
        scratch_shapes=[
            pltpu.VMEM((total, 2 * BLK), F32),
            pltpu.VMEM((slots * BLK, wide), F32),
            pltpu.VMEM((slots * BLK, wide), F32),
            pltpu.VMEM((total, BLK), F32),
            pltpu.VMEM((wide, BLK), BF16),
            pltpu.VMEM((wide, BLK), BF16),
            pltpu.VMEM((BLK, wide), F32),
        ],
        compiler_params=pltpu.CompilerParams(vmem_limit_bytes=56 * 2**20),
        name="attend",
    )(listed, q, do, kv_all, own)


def on_device(devices, query, key, value, d_mixed, out_weight, block_keys, scope_ids):
    tokens, heads, width = query.shape
    kv = key.shape[1]
    cols = 2 * kv * width
    scope_rows = jnp.zeros((PAD, cols), BF16).at[:, :tokens].set(scope_ids.astype(BF16)[None, :])
    block = jnp.concatenate(
        [
            jnp.concatenate([key.reshape(tokens, -1), value.reshape(tokens, -1)], axis=1),
            scope_rows,
        ],
        axis=0,
    )
    kv_all = lax.all_gather(block, "ctx", axis=0, tiled=True)
    d_out = lax.dot_general(
        lax.all_gather(d_mixed, "head", axis=1, tiled=True),
        out_weight,
        NT,
        preferred_element_type=F32,
    ).astype(BF16)
    own = scope_ids.astype(F32).reshape(tokens // BLK, BLK)
    grad_q, part = attend(
        block_keys, query.reshape(tokens, -1), d_out, kv_all, own, devices, kv
    )
    home = lax.psum_scatter(part, "ctx", scatter_dimension=0, tiled=True)
    half = kv * width
    return (
        grad_q.reshape(query.shape),
        home[:, :half].reshape(key.shape),
        home[:, half:].reshape(value.shape),
    )


def solution(mesh):
    in_specs = (
        P("ctx", "head", None),
        P("ctx", "head", None),
        P("ctx", "head", None),
        P("ctx", "head"),
        P("head", None),
        P("ctx", None),
        P("ctx"),
    )
    out_specs = (P("ctx", "head", None), P("ctx", "head", None), P("ctx", "head", None))
    return jax.shard_map(
        functools.partial(on_device, mesh.shape["ctx"]),
        mesh=mesh,
        in_specs=in_specs,
        out_specs=out_specs,
        check_vma=False,
    )
```

```python
import functools
import math

import jax
import jax.numpy as jnp
from jax import lax
from jax.experimental import pallas as pl
from jax.experimental.pallas import tpu as pltpu
from jax.sharding import PartitionSpec as P

BLK = 128
PAD = 16
F32 = jnp.float32
BF16 = jnp.bfloat16
NT = (((1,), (1,)), ((), ()))
TN = (((0,), (0,)), ((), ()))
MESH = pl.DeviceIdType.MESH


def attend_kernel(
    devices, tokens, kv, group, slots, listed, q_ref, do_ref, kv_ref, own_ref, gq_ref, part_ref,
    acc, s_scr, dp_scr, scope_scr, qg, dg, gq_acc,
):
    blocks = tokens // BLK
    width = BLK
    wide = group * BLK
    cut = next(c for c in (4, 2, 1) if slots % c == 0)
    chunk = cut * BLK
    scale = 1.0 / math.sqrt(width)
    log2e = scale * math.log2(math.e)

    def fill(d, _):
        tile = kv_ref[pl.ds(pl.multiple_of(d * (tokens + PAD) + tokens, PAD), PAD), 0:tokens]
        for b in range(blocks):
            row = tile[0:1, b * BLK : (b + 1) * BLK].astype(F32)
            at = pl.multiple_of((d * blocks + b) * BLK, BLK)
            scope_scr[pl.ds(at, BLK), :] = jnp.broadcast_to(row, (BLK, BLK)).T
        return 0

    lax.fori_loop(0, devices, fill, 0)

    def rows_of(j):
        d = j // blocks
        return pl.ds(pl.multiple_of(d * (tokens + PAD) + (j - d * blocks) * BLK, PAD), BLK)

    def head_loop(g, _):
        k_cols = pl.ds(pl.multiple_of(g * width, width), width)
        v_cols = pl.ds(pl.multiple_of((kv + g) * width, width), width)
        acc[...] = jnp.zeros_like(acc)

        def row_loop(r, _):
            q_rows = pl.ds(pl.multiple_of(r * BLK, BLK), BLK)

            def head_cols(n):
                return pl.ds(pl.multiple_of((g * group + n) * width, width), width)

            for n in range(group):
                qg[n * BLK : (n + 1) * BLK, :] = q_ref[q_rows, head_cols(n)]
                dg[n * BLK : (n + 1) * BLK, :] = do_ref[q_rows, head_cols(n)]
            own = own_ref[pl.ds(r, 1), :]

            def listed_rows(c):
                return [listed[r, c * cut + u] for u in range(cut)]

            def near(c, cols):
                return jnp.concatenate([kv_ref[rows_of(j), cols] for j in listed_rows(c)], axis=0)

            def here(c):
                return pl.ds(pl.multiple_of(c * chunk, chunk), chunk)

            def first(c, high):
                s = lax.dot_general(near(c, k_cols), qg[...], NT, preferred_element_type=F32)
                bias = []
                for j in listed_rows(c):
                    sk = scope_scr[pl.ds(pl.multiple_of(j * BLK, BLK), BLK), :]
                    b = jnp.where((sk == own) | (sk == 0.0), 0.0, -1e30)
                    bias.append(jnp.concatenate([b] * group, axis=1))
                s = s + jnp.concatenate(bias, axis=0)
                s_scr[here(c), :] = s
                return jnp.maximum(high, jnp.max(s, axis=0, keepdims=True))

            high = lax.fori_loop(0, slots // cut, first, jnp.full((1, wide), -1e30, F32))

            def second(c, carry):
                total, delta = carry
                p = jnp.exp2((s_scr[here(c), :] - high) * log2e)
                dp = lax.dot_general(near(c, v_cols), dg[...], NT, preferred_element_type=F32)
                s_scr[here(c), :] = p
                dp_scr[here(c), :] = dp
                return (
                    total + jnp.sum(p, axis=0, keepdims=True),
                    delta + jnp.sum(p * dp, axis=0, keepdims=True),
                )

            zero = jnp.zeros((1, wide), F32)
            total, delta = lax.fori_loop(0, slots // cut, second, (zero, zero))
            inverse = 1.0 / total
            delta = delta * inverse
            gq_acc[...] = jnp.zeros_like(gq_acc)

            def third(c, _):
                pn = s_scr[here(c), :] * inverse
                ds = (pn * ((dp_scr[here(c), :] - delta) * scale)).astype(BF16)
                gv = jnp.dot(pn.astype(BF16), dg[...], preferred_element_type=F32)
                gk = jnp.dot(ds, qg[...], preferred_element_type=F32)
                gq_acc[...] += lax.dot_general(near(c, k_cols), ds, TN, preferred_element_type=F32)
                for u, j in enumerate(listed_rows(c)):
                    at = pl.ds(pl.multiple_of(j * BLK, BLK), BLK)
                    acc[at, 0:width] += gk[u * BLK : (u + 1) * BLK, :]
                    acc[at, width : 2 * width] += gv[u * BLK : (u + 1) * BLK, :]
                return 0

            lax.fori_loop(0, slots // cut, third, 0)
            for n in range(group):
                gq_ref[q_rows, head_cols(n)] = gq_acc[:, n * BLK : (n + 1) * BLK].T.astype(BF16)
            return 0

        lax.fori_loop(0, blocks, row_loop, 0)
        part_ref[:, k_cols] = acc[:, 0:width].astype(BF16)
        part_ref[:, v_cols] = acc[:, width : 2 * width].astype(BF16)
        return 0

    lax.fori_loop(0, kv, head_loop, 0)


def attend(listed, q, do, kv_all, own, devices, kv):
    tokens = q.shape[0]
    group = q.shape[1] // BLK // kv
    slots = listed.shape[1]
    total = devices * tokens
    wide = group * BLK
    vmem = pl.BlockSpec(memory_space=pltpu.VMEM)
    return pl.pallas_call(
        functools.partial(attend_kernel, devices, tokens, kv, group, slots),
        out_shape=(
            jax.ShapeDtypeStruct(q.shape, BF16),
            jax.ShapeDtypeStruct((total, 2 * kv * BLK), BF16),
        ),
        in_specs=[pl.BlockSpec(memory_space=pltpu.SMEM)] + [vmem] * 4,
        out_specs=(vmem, vmem),
        scratch_shapes=[
            pltpu.VMEM((total, 2 * BLK), F32),
            pltpu.VMEM((slots * BLK, wide), F32),
            pltpu.VMEM((slots * BLK, wide), F32),
            pltpu.VMEM((total, BLK), F32),
            pltpu.VMEM((wide, BLK), BF16),
            pltpu.VMEM((wide, BLK), BF16),
            pltpu.VMEM((BLK, wide), F32),
        ],
        compiler_params=pltpu.CompilerParams(vmem_limit_bytes=56 * 2**20),
        name="attend",
    )(listed, q, do, kv_all, own)


def place(devices):
    me = lax.axis_index("ctx")
    a, b, c = me // 4, lax.rem(me // 2, 2), lax.rem(me, 2)
    return a, b, c, devices // 4


def greet(ctx_peers, head_peers):
    barrier = pltpu.get_barrier_semaphore()
    for peer in ctx_peers:
        pl.semaphore_signal(barrier, inc=1, device_id={"ctx": peer}, device_id_type=MESH)
    for peer in head_peers:
        pl.semaphore_signal(barrier, inc=1, device_id={"head": peer}, device_id_type=MESH)
    pl.semaphore_wait(barrier, len(ctx_peers) + len(head_peers))


def near_first(count):
    return sorted(range(1, count), key=lambda o: min(o, count - o))


def gather_kernel(
    devices, heads, block_ref, mixed_ref, all_ref, wide_ref,
    z_send, z_recv, x_send, x_recv, c_send, c_recv, h_send, h_recv, own_sem,
):
    rows = block_ref.shape[0]
    width = mixed_ref.shape[1]
    a, b, c, count = place(devices)
    head = lax.axis_index("head")
    order = near_first(count)

    def index(o, far, other):
        far_a = lax.rem(a - o + count, count)
        return far_a * 4 + ((1 - b) if far else b) * 2 + ((1 - c) if other else c)

    def slot(i):
        return all_ref.at[pl.ds(pl.multiple_of(i * rows, PAD), rows)]

    def cols(h):
        return wide_ref.at[:, pl.ds(pl.multiple_of(h * width, BLK), width)]

    z_peers = {o: lax.rem(a + o, count) * 4 + b * 2 + c for o in order}
    x_peer = a * 4 + (1 - b) * 2 + c
    c_peer = a * 4 + b * 2 + (1 - c)
    h_peers = {o: lax.rem(head + o, heads) for o in range(1, heads)}
    greet([z_peers[o] for o in order] + [x_peer, c_peer], list(h_peers.values()))

    def copy(src, dst, send, recv, where):
        return pltpu.make_async_remote_copy(
            src_ref=src, dst_ref=dst, send_sem=send, recv_sem=recv,
            device_id=where, device_id_type=MESH,
        )

    sent = []

    def send(*args):
        out = copy(*args)
        out.start()
        sent.append(out)

    mine = slot(index(0, False, False))
    keep = pltpu.make_async_copy(block_ref, mine, own_sem.at[0])
    keep.start()
    keep_mixed = pltpu.make_async_copy(mixed_ref, cols(head), own_sem.at[1])
    keep_mixed.start()
    send(block_ref, mine, x_send.at[0], x_recv.at[0], {"ctx": x_peer})
    for o in order:
        send(block_ref, mine, z_send.at[o], z_recv.at[o], {"ctx": z_peers[o]})
    for o in range(1, heads):
        send(mixed_ref, cols(head), h_send.at[o], h_recv.at[o], {"head": h_peers[o]})
    send(block_ref, mine, c_send.at[0], c_recv.at[0], {"ctx": c_peer})

    def arrived(ref, sem, where):
        copy(ref, ref, own_sem.at[2], sem, where).wait_recv()

    def over_x(o):
        got = slot(index(o, True, False))
        arrived(got, x_recv.at[o], {"ctx": x_peer})
        at = 2 * o + 1
        send(got, got, c_send.at[at], c_recv.at[at], {"ctx": c_peer})

    before = 0
    for o in order:
        got = slot(index(o, False, False))
        arrived(got, z_recv.at[o], {"ctx": z_peers[o]})
        send(got, got, x_send.at[o], x_recv.at[o], {"ctx": x_peer})
        send(got, got, c_send.at[2 * o], c_recv.at[2 * o], {"ctx": c_peer})
        over_x(before)
        before = o
    over_x(before)
    for o in range(count):
        for far in (False, True):
            at = 2 * o + int(far)
            arrived(slot(index(o, far, True)), c_recv.at[at], {"ctx": c_peer})
    for o in range(1, heads):
        arrived(cols(lax.rem(head - o + heads, heads)), h_recv.at[o], {"head": h_peers[o]})
    for out in sent:
        out.wait_send()
    keep.wait()
    keep_mixed.wait()


def gather(block, d_mixed, devices, heads):
    count = devices // 4
    dma = pltpu.SemaphoreType.DMA
    hbm = pl.BlockSpec(memory_space=pl.ANY)
    return pl.pallas_call(
        functools.partial(gather_kernel, devices, heads),
        out_shape=(
            jax.ShapeDtypeStruct((devices * block.shape[0], block.shape[1]), BF16),
            jax.ShapeDtypeStruct((d_mixed.shape[0], heads * d_mixed.shape[1]), BF16),
        ),
        in_specs=[hbm, hbm],
        out_specs=(hbm, hbm),
        scratch_shapes=[
            dma((count,)), dma((count,)), dma((count,)), dma((count,)),
            dma((2 * count,)), dma((2 * count,)), dma((heads,)), dma((heads,)), dma((3,)),
        ],
        compiler_params=pltpu.CompilerParams(collective_id=0, has_side_effects=True),
        name="gather",
    )(block, d_mixed)


def scatter_kernel(
    devices, part_ref, home_ref, c_land, x_land, z_land, x_out, z_out,
    c_send, c_recv, x_send, x_recv, z_send, z_recv,
):
    rows = home_ref.shape[0]
    step = 32
    a, b, c, count = place(devices)
    order = near_first(count)[::-1] + [0]

    def part_at(o, far, other):
        i = lax.rem(a + o, count) * 4 + ((1 - b) if far else b) * 2 + ((1 - c) if other else c)
        return pl.multiple_of(i * rows, rows)

    z_peers = {o: lax.rem(a + o, count) * 4 + b * 2 + c for o in range(1, count)}
    x_peer = a * 4 + (1 - b) * 2 + c
    c_peer = a * 4 + b * 2 + (1 - c)
    greet(list(z_peers.values()) + [x_peer, c_peer], [])

    def copy(src, dst, send, recv, peer):
        return pltpu.make_async_remote_copy(
            src_ref=src, dst_ref=dst, send_sem=send, recv_sem=recv,
            device_id={"ctx": peer}, device_id_type=MESH,
        )

    core, across, along = {}, {}, {}
    for far in (True, False):
        for o in order:
            at = 2 * o + int(far)
            core[at] = copy(
                part_ref.at[pl.ds(part_at(o, far, True), rows)], c_land.at[at],
                c_send.at[at], c_recv.at[at], c_peer,
            )
            core[at].start()

    def add(out, at, terms):
        def body(i, _):
            here = pl.multiple_of(i * step, step)
            total = part_ref[pl.ds(at + here, step), :].astype(F32)
            for land, index in terms:
                total = total + land[index, pl.ds(here, step), :].astype(F32)
            out[pl.ds(here, step), :] = total.astype(BF16)
            return 0

        lax.fori_loop(0, rows // step, body, 0)

    for o in order:
        at = 2 * o + 1
        core[at].wait_recv()
        add(x_out.at[o], part_at(o, True, False), [(c_land, at)])
        across[o] = copy(x_out.at[o], x_land.at[o], x_send.at[o], x_recv.at[o], x_peer)
        across[o].start()
    for o in order:
        core[2 * o].wait_recv()
        across[o].wait_recv()
        terms = [(c_land, 2 * o), (x_land, o)]
        if o > 0:
            add(z_out.at[o], part_at(o, False, False), terms)
            along[o] = copy(z_out.at[o], z_land.at[o], z_send.at[o], z_recv.at[o], z_peers[o])
            along[o].start()
    for o in order[:-1]:
        along[o].wait_recv()
    add(
        home_ref,
        part_at(0, False, False),
        [(c_land, 0), (x_land, 0)] + [(z_land, o) for o in range(1, count)],
    )
    for made in (core, across, along):
        for out in made.values():
            out.wait_send()


def scatter(part, devices):
    count = devices // 4
    dma = pltpu.SemaphoreType.DMA
    vmem = pl.BlockSpec(memory_space=pltpu.VMEM)
    block = (part.shape[0] // devices, part.shape[1])
    return pl.pallas_call(
        functools.partial(scatter_kernel, devices),
        out_shape=jax.ShapeDtypeStruct(block, BF16),
        in_specs=[vmem],
        out_specs=vmem,
        scratch_shapes=[
            pltpu.VMEM((2 * count,) + block, BF16),
            pltpu.VMEM((count,) + block, BF16),
            pltpu.VMEM((count,) + block, BF16),
            pltpu.VMEM((count,) + block, BF16),
            pltpu.VMEM((count,) + block, BF16),
            dma((2 * count,)), dma((2 * count,)),
            dma((count,)), dma((count,)), dma((count,)), dma((count,)),
        ],
        compiler_params=pltpu.CompilerParams(
            collective_id=1, has_side_effects=True, vmem_limit_bytes=40 * 2**20
        ),
        name="scatter",
    )(part)


def on_device(devices, split, query, key, value, d_mixed, out_weight, block_keys, scope_ids):
    tokens, heads, width = query.shape
    kv = key.shape[1]
    cols = 2 * kv * width
    scope_rows = jnp.zeros((PAD, cols), BF16).at[:, :tokens].set(scope_ids.astype(BF16)[None, :])
    block = jnp.concatenate(
        [
            jnp.concatenate([key.reshape(tokens, -1), value.reshape(tokens, -1)], axis=1),
            scope_rows,
        ],
        axis=0,
    )
    kv_all, mixed = gather(block, d_mixed, devices, split)
    d_out = lax.dot_general(
        mixed,
        out_weight,
        NT,
        preferred_element_type=F32,
    ).astype(BF16)
    own = scope_ids.astype(F32).reshape(tokens // BLK, BLK)
    grad_q, part = attend(
        block_keys, query.reshape(tokens, -1), d_out, kv_all, own, devices, kv
    )
    home = scatter(part, devices)
    half = kv * width
    return (
        grad_q.reshape(query.shape),
        home[:, :half].reshape(key.shape),
        home[:, half:].reshape(value.shape),
    )


def solution(mesh):
    in_specs = (
        P("ctx", "head", None),
        P("ctx", "head", None),
        P("ctx", "head", None),
        P("ctx", "head"),
        P("head", None),
        P("ctx", None),
        P("ctx"),
    )
    out_specs = (P("ctx", "head", None), P("ctx", "head", None), P("ctx", "head", None))
    return jax.shard_map(
        functools.partial(on_device, mesh.shape["ctx"], mesh.shape["head"]),
        mesh=mesh,
        in_specs=in_specs,
        out_specs=out_specs,
        check_vma=False,
    )
```

```python
import functools
import math

import jax
import jax.numpy as jnp
from jax import lax
from jax.experimental import pallas as pl
from jax.experimental.pallas import tpu as pltpu
from jax.sharding import PartitionSpec as P

BLK = 128
PAD = 16
F32 = jnp.float32
BF16 = jnp.bfloat16
NT = (((1,), (1,)), ((), ()))
TN = (((0,), (0,)), ((), ()))
MESH = pl.DeviceIdType.MESH


def attend_kernel(
    devices, tokens, kv, group, slots, listed, q_ref, do_ref, kv_ref, own_ref, gq_ref, part_ref,
    acc, s_scr, dp_scr, scope_scr, qg, dg, gq_acc,
):
    blocks = tokens // BLK
    width = BLK
    wide = group * BLK
    cut = next(c for c in (4, 2, 1) if slots % c == 0)
    chunk = cut * BLK
    scale = 1.0 / math.sqrt(width)
    log2e = scale * math.log2(math.e)

    def fill(d, _):
        tile = kv_ref[pl.ds(pl.multiple_of(d * (tokens + PAD) + tokens, PAD), PAD), 0:tokens]
        for b in range(blocks):
            row = tile[0:1, b * BLK : (b + 1) * BLK].astype(F32)
            at = pl.multiple_of((d * blocks + b) * BLK, BLK)
            scope_scr[pl.ds(at, BLK), :] = jnp.broadcast_to(row, (BLK, BLK)).T
        return 0

    lax.fori_loop(0, devices, fill, 0)

    def rows_of(j):
        d = j // blocks
        return pl.ds(pl.multiple_of(d * (tokens + PAD) + (j - d * blocks) * BLK, PAD), BLK)

    def head_loop(g, _):
        k_cols = pl.ds(pl.multiple_of(g * width, width), width)
        v_cols = pl.ds(pl.multiple_of((kv + g) * width, width), width)
        acc[...] = jnp.zeros_like(acc)

        def row_loop(r, _):
            q_rows = pl.ds(pl.multiple_of(r * BLK, BLK), BLK)

            def head_cols(n):
                return pl.ds(pl.multiple_of((g * group + n) * width, width), width)

            for n in range(group):
                qg[n * BLK : (n + 1) * BLK, :] = q_ref[q_rows, head_cols(n)]
                dg[n * BLK : (n + 1) * BLK, :] = do_ref[q_rows, head_cols(n)]
            own = own_ref[pl.ds(r, 1), :]

            def listed_rows(c):
                return [listed[r, c * cut + u] for u in range(cut)]

            def near(c, cols):
                return jnp.concatenate([kv_ref[rows_of(j), cols] for j in listed_rows(c)], axis=0)

            def here(c):
                return pl.ds(pl.multiple_of(c * chunk, chunk), chunk)

            def first(c, high):
                s = lax.dot_general(near(c, k_cols), qg[...], NT, preferred_element_type=F32)
                bias = []
                for j in listed_rows(c):
                    sk = scope_scr[pl.ds(pl.multiple_of(j * BLK, BLK), BLK), :]
                    b = jnp.where((sk == own) | (sk == 0.0), 0.0, -1e30)
                    bias.append(jnp.concatenate([b] * group, axis=1))
                s = s + jnp.concatenate(bias, axis=0)
                s_scr[here(c), :] = s
                return jnp.maximum(high, jnp.max(s, axis=0, keepdims=True))

            high = lax.fori_loop(0, slots // cut, first, jnp.full((1, wide), -1e30, F32))

            def second(c, carry):
                total, delta = carry
                p = jnp.exp2((s_scr[here(c), :] - high) * log2e)
                dp = lax.dot_general(near(c, v_cols), dg[...], NT, preferred_element_type=F32)
                s_scr[here(c), :] = p
                dp_scr[here(c), :] = dp
                return (
                    total + jnp.sum(p, axis=0, keepdims=True),
                    delta + jnp.sum(p * dp, axis=0, keepdims=True),
                )

            zero = jnp.zeros((1, wide), F32)
            total, delta = lax.fori_loop(0, slots // cut, second, (zero, zero))
            inverse = 1.0 / total
            delta = delta * inverse
            gq_acc[...] = jnp.zeros_like(gq_acc)

            def third(c, _):
                pn = s_scr[here(c), :] * inverse
                ds = (pn * ((dp_scr[here(c), :] - delta) * scale)).astype(BF16)
                gv = jnp.dot(pn.astype(BF16), dg[...], preferred_element_type=F32)
                gk = jnp.dot(ds, qg[...], preferred_element_type=F32)
                gq_acc[...] += lax.dot_general(near(c, k_cols), ds, TN, preferred_element_type=F32)
                for u, j in enumerate(listed_rows(c)):
                    at = pl.ds(pl.multiple_of(j * BLK, BLK), BLK)
                    acc[at, 0:width] += gk[u * BLK : (u + 1) * BLK, :]
                    acc[at, width : 2 * width] += gv[u * BLK : (u + 1) * BLK, :]
                return 0

            lax.fori_loop(0, slots // cut, third, 0)
            for n in range(group):
                gq_ref[q_rows, head_cols(n)] = gq_acc[:, n * BLK : (n + 1) * BLK].T.astype(BF16)
            return 0

        lax.fori_loop(0, blocks, row_loop, 0)
        part_ref[:, k_cols] = acc[:, 0:width].astype(BF16)
        part_ref[:, v_cols] = acc[:, width : 2 * width].astype(BF16)
        return 0

    lax.fori_loop(0, kv, head_loop, 0)


def attend(listed, q, do, kv_all, own, devices, kv):
    tokens = q.shape[0]
    group = q.shape[1] // BLK // kv
    slots = listed.shape[1]
    total = devices * tokens
    wide = group * BLK
    vmem = pl.BlockSpec(memory_space=pltpu.VMEM)
    return pl.pallas_call(
        functools.partial(attend_kernel, devices, tokens, kv, group, slots),
        out_shape=(
            jax.ShapeDtypeStruct(q.shape, BF16),
            jax.ShapeDtypeStruct((total, 2 * kv * BLK), BF16),
        ),
        in_specs=[pl.BlockSpec(memory_space=pltpu.SMEM)] + [vmem] * 4,
        out_specs=(vmem, vmem),
        scratch_shapes=[
            pltpu.VMEM((total, 2 * BLK), F32),
            pltpu.VMEM((slots * BLK, wide), F32),
            pltpu.VMEM((slots * BLK, wide), F32),
            pltpu.VMEM((total, BLK), F32),
            pltpu.VMEM((wide, BLK), BF16),
            pltpu.VMEM((wide, BLK), BF16),
            pltpu.VMEM((BLK, wide), F32),
        ],
        compiler_params=pltpu.CompilerParams(vmem_limit_bytes=56 * 2**20),
        name="attend",
    )(listed, q, do, kv_all, own)


def place(devices):
    me = lax.axis_index("ctx")
    a, b, c = me // 4, lax.rem(me // 2, 2), lax.rem(me, 2)
    return a, b, c, devices // 4


def greet(ctx_peers, head_peers):
    barrier = pltpu.get_barrier_semaphore()
    for peer in ctx_peers:
        pl.semaphore_signal(barrier, inc=1, device_id={"ctx": peer}, device_id_type=MESH)
    for peer in head_peers:
        pl.semaphore_signal(barrier, inc=1, device_id={"head": peer}, device_id_type=MESH)
    pl.semaphore_wait(barrier, len(ctx_peers) + len(head_peers))


def near_first(count):
    return sorted(range(1, count), key=lambda o: min(o, count - o))


def gather_kernel(
    devices, heads, block_ref, mixed_ref, weight_ref, all_ref, do_ref, wide, weight,
    z_send, z_recv, x_send, x_recv, c_send, c_recv, h_send, h_recv, own_sem,
):
    rows = block_ref.shape[0]
    width = mixed_ref.shape[1]
    a, b, c, count = place(devices)
    head = lax.axis_index("head")
    x_peer = a * 4 + (1 - b) * 2 + c
    c_peer = a * 4 + b * 2 + (1 - c)
    h_peers = {o: lax.rem(head + o, heads) for o in range(1, heads)}

    def slot(at, far, other):
        i = at * 4 + ((1 - b) if far else b) * 2 + ((1 - c) if other else c)
        return all_ref.at[pl.ds(pl.multiple_of(i * rows, PAD), rows)]

    def cols(h):
        return wide.at[:, pl.ds(pl.multiple_of(h * width, BLK), width)]

    barrier = pltpu.get_barrier_semaphore()
    for way in (1, -1):

        @pl.when((a + way >= 0) & (a + way < count))
        def _():
            pl.semaphore_signal(
                barrier, inc=1, device_id={"ctx": (a + way) * 4 + b * 2 + c}, device_id_type=MESH
            )

    for peer in (x_peer, c_peer):
        pl.semaphore_signal(barrier, inc=1, device_id={"ctx": peer}, device_id_type=MESH)
    for peer in h_peers.values():
        pl.semaphore_signal(barrier, inc=1, device_id={"head": peer}, device_id_type=MESH)
    inner = jnp.where((a > 0) & (a < count - 1), 1, 0)
    pl.semaphore_wait(barrier, 3 + len(h_peers) + inner)

    def copy(src, dst, send, recv, where):
        return pltpu.make_async_remote_copy(
            src_ref=src, dst_ref=dst, send_sem=send, recv_sem=recv,
            device_id=where, device_id_type=MESH,
        )

    def along(src, at, way, s):
        n = (0 if way > 0 else count) + s
        peer = (a + way) * 4 + b * 2 + c
        return copy(src, slot(at, False, False), z_send.at[n], z_recv.at[n], {"ctx": peer})

    def across(src, at):
        return copy(src, slot(at, False, False), x_send.at[at], x_recv.at[at], {"ctx": x_peer})

    def core(src, at, far):
        n = 2 * at + int(far)
        return copy(src, slot(at, far, False), c_send.at[n], c_recv.at[n], {"ctx": c_peer})

    def valid(at):
        return (at >= 0) & (at < count)

    load = pltpu.make_async_copy(weight_ref, weight, own_sem.at[2])
    load.start()
    keep = pltpu.make_async_copy(block_ref, slot(a, False, False), own_sem.at[0])
    keep.start()
    keep_mixed = pltpu.make_async_copy(mixed_ref, cols(head), own_sem.at[1])
    keep_mixed.start()
    across(block_ref, a).start()
    for way in (1, -1):

        @pl.when(valid(a + way))
        def _():
            along(block_ref, a, way, 0).start()

    to_head = {
        o: copy(mixed_ref, cols(head), h_send.at[o], h_recv.at[o], {"head": h_peers[o]})
        for o in h_peers
    }
    for out in to_head.values():
        out.start()
    core(block_ref, a, False).start()

    def over_x(at):
        got = slot(at, True, False)
        copy(got, got, x_send.at[at], x_recv.at[at], {"ctx": x_peer}).wait_recv()
        core(got, at, True).start()

    def over_x_of(s):
        for way in (1, -1):

            @pl.when(valid(a - way * s))
            def _():
                over_x(a - way * s)

    tile = 2 * BLK if weight.shape[0] % (2 * BLK) == 0 else BLK
    tiles = weight.shape[0] // tile
    edges = [tiles * t // (count - 1) for t in range(count)]

    def project(t, _):
        at = pl.multiple_of(t * tile, tile)
        made = lax.dot_general(
            wide[...], weight[pl.ds(at, tile), :], NT, preferred_element_type=F32
        )
        do_ref[:, pl.ds(at, tile)] = made.astype(BF16)
        return 0

    for s in range(1, count):
        for way in (1, -1):
            at = a - way * s

            @pl.when(valid(at))
            def _():
                got = slot(at, False, False)
                n = (0 if way > 0 else count) + s - 1
                peer = {"ctx": (a - way) * 4 + b * 2 + c}
                copy(got, got, z_send.at[n], z_recv.at[n], peer).wait_recv()

                @pl.when(valid(a + way))
                def _():
                    along(got, at, way, s).start()

                across(got, at).start()
                core(got, at, False).start()

        if s == 1:
            over_x(a)
        else:
            over_x_of(s - 1)
        if s == min(2, count - 1):
            keep_mixed.wait()
            load.wait()
            for o in h_peers:
                to = cols(lax.rem(head - o + heads, heads))
                copy(to, to, h_send.at[o], h_recv.at[o], {"head": h_peers[o]}).wait_recv()
            lax.fori_loop(0, edges[s], project, 0)
        elif s > 2:
            lax.fori_loop(edges[s - 1], edges[s], project, 0)
    over_x_of(count - 1)
    for at in range(count):
        for far in (False, True):
            n = 2 * at + int(far)
            got = slot(at, far, True)
            copy(got, got, c_send.at[n], c_recv.at[n], {"ctx": c_peer}).wait_recv()
    keep.wait()
    for out in to_head.values():
        out.wait_send()
    for way in (1, -1):
        for s in range(count - 1):

            @pl.when(valid(a - way * s) & valid(a + way))
            def _():
                at = a - way * s
                along(slot(at, False, False), at, way, s).wait_send()

    for at in range(count):
        across(slot(at, False, False), at).wait_send()
        for far in (False, True):
            core(slot(at, far, False), at, far).wait_send()


def gather(block, d_mixed, weight, devices, heads):
    count = devices // 4
    dma = pltpu.SemaphoreType.DMA
    hbm = pl.BlockSpec(memory_space=pl.ANY)
    tokens = d_mixed.shape[0]
    return pl.pallas_call(
        functools.partial(gather_kernel, devices, heads),
        out_shape=(
            jax.ShapeDtypeStruct((devices * block.shape[0], block.shape[1]), BF16),
            jax.ShapeDtypeStruct((tokens, weight.shape[0]), BF16),
        ),
        in_specs=[hbm, hbm, hbm],
        out_specs=(hbm, pl.BlockSpec(memory_space=pltpu.VMEM)),
        scratch_shapes=[
            pltpu.VMEM((tokens, heads * d_mixed.shape[1]), BF16),
            pltpu.VMEM(weight.shape, BF16),
            dma((2 * count,)), dma((2 * count,)), dma((count,)), dma((count,)),
            dma((2 * count,)), dma((2 * count,)), dma((heads,)), dma((heads,)), dma((3,)),
        ],
        compiler_params=pltpu.CompilerParams(
            collective_id=0, has_side_effects=True, vmem_limit_bytes=48 * 2**20
        ),
        name="gather",
    )(block, d_mixed, weight)


def scatter_kernel(
    devices, part_ref, home_ref, c_land, x_land, z_land, x_out, z_out,
    c_send, c_recv, x_send, x_recv, z_send, z_recv,
):
    rows = home_ref.shape[0]
    step = 32
    a, b, c, count = place(devices)
    order = near_first(count)[::-1] + [0]

    def part_at(o, far, other):
        i = lax.rem(a + o, count) * 4 + ((1 - b) if far else b) * 2 + ((1 - c) if other else c)
        return pl.multiple_of(i * rows, rows)

    z_peers = {o: lax.rem(a + o, count) * 4 + b * 2 + c for o in range(1, count)}
    x_peer = a * 4 + (1 - b) * 2 + c
    c_peer = a * 4 + b * 2 + (1 - c)
    greet(list(z_peers.values()) + [x_peer, c_peer], [])

    def copy(src, dst, send, recv, peer):
        return pltpu.make_async_remote_copy(
            src_ref=src, dst_ref=dst, send_sem=send, recv_sem=recv,
            device_id={"ctx": peer}, device_id_type=MESH,
        )

    core, across, along = {}, {}, {}
    for far in (True, False):
        for o in order:
            at = 2 * o + int(far)
            core[at] = copy(
                part_ref.at[pl.ds(part_at(o, far, True), rows)], c_land.at[at],
                c_send.at[at], c_recv.at[at], c_peer,
            )
            core[at].start()

    def add(out, at, terms):
        def body(i, _):
            here = pl.multiple_of(i * step, step)
            total = part_ref[pl.ds(at + here, step), :].astype(F32)
            for land, index in terms:
                total = total + land[index, pl.ds(here, step), :].astype(F32)
            out[pl.ds(here, step), :] = total.astype(BF16)
            return 0

        lax.fori_loop(0, rows // step, body, 0)

    for o in order:
        at = 2 * o + 1
        core[at].wait_recv()
        add(x_out.at[o], part_at(o, True, False), [(c_land, at)])
        across[o] = copy(x_out.at[o], x_land.at[o], x_send.at[o], x_recv.at[o], x_peer)
        across[o].start()
    for o in order:
        core[2 * o].wait_recv()
        across[o].wait_recv()
        terms = [(c_land, 2 * o), (x_land, o)]
        if o > 0:
            add(z_out.at[o], part_at(o, False, False), terms)
            along[o] = copy(z_out.at[o], z_land.at[o], z_send.at[o], z_recv.at[o], z_peers[o])
            along[o].start()
    for o in order[:-1]:
        along[o].wait_recv()
    add(
        home_ref,
        part_at(0, False, False),
        [(c_land, 0), (x_land, 0)] + [(z_land, o) for o in range(1, count)],
    )
    for made in (core, across, along):
        for out in made.values():
            out.wait_send()


def scatter(part, devices):
    count = devices // 4
    dma = pltpu.SemaphoreType.DMA
    vmem = pl.BlockSpec(memory_space=pltpu.VMEM)
    block = (part.shape[0] // devices, part.shape[1])
    return pl.pallas_call(
        functools.partial(scatter_kernel, devices),
        out_shape=jax.ShapeDtypeStruct(block, BF16),
        in_specs=[vmem],
        out_specs=vmem,
        scratch_shapes=[
            pltpu.VMEM((2 * count,) + block, BF16),
            pltpu.VMEM((count,) + block, BF16),
            pltpu.VMEM((count,) + block, BF16),
            pltpu.VMEM((count,) + block, BF16),
            pltpu.VMEM((count,) + block, BF16),
            dma((2 * count,)), dma((2 * count,)),
            dma((count,)), dma((count,)), dma((count,)), dma((count,)),
        ],
        compiler_params=pltpu.CompilerParams(
            collective_id=1, has_side_effects=True, vmem_limit_bytes=40 * 2**20
        ),
        name="scatter",
    )(part)


def on_device(devices, split, query, key, value, d_mixed, out_weight, block_keys, scope_ids):
    tokens, heads, width = query.shape
    kv = key.shape[1]
    cols = 2 * kv * width
    scope_rows = jnp.zeros((PAD, cols), BF16).at[:, :tokens].set(scope_ids.astype(BF16)[None, :])
    block = jnp.concatenate(
        [
            jnp.concatenate([key.reshape(tokens, -1), value.reshape(tokens, -1)], axis=1),
            scope_rows,
        ],
        axis=0,
    )
    kv_all, d_out = gather(block, d_mixed, out_weight, devices, split)
    own = scope_ids.astype(F32).reshape(tokens // BLK, BLK)
    grad_q, part = attend(
        block_keys, query.reshape(tokens, -1), d_out, kv_all, own, devices, kv
    )
    home = scatter(part, devices)
    half = kv * width
    return (
        grad_q.reshape(query.shape),
        home[:, :half].reshape(key.shape),
        home[:, half:].reshape(value.shape),
    )


def solution(mesh):
    in_specs = (
        P("ctx", "head", None),
        P("ctx", "head", None),
        P("ctx", "head", None),
        P("ctx", "head"),
        P("head", None),
        P("ctx", None),
        P("ctx"),
    )
    out_specs = (P("ctx", "head", None), P("ctx", "head", None), P("ctx", "head", None))
    return jax.shard_map(
        functools.partial(on_device, mesh.shape["ctx"], mesh.shape["head"]),
        mesh=mesh,
        in_specs=in_specs,
        out_specs=out_specs,
        check_vma=False,
    )
```

```python
import functools
import math

import jax
import jax.numpy as jnp
from jax import lax
from jax.experimental import pallas as pl
from jax.experimental.pallas import tpu as pltpu
from jax.sharding import PartitionSpec as P

BLK = 128
PAD = 16
F32 = jnp.float32
BF16 = jnp.bfloat16
NT = (((1,), (1,)), ((), ()))
TN = (((0,), (0,)), ((), ()))
MESH = pl.DeviceIdType.MESH


def attend_kernel(
    devices, tokens, kv, group, slots, listed, q_ref, do_ref, kv_ref, own_ref, gq_ref, part_ref,
    acc, s_scr, dp_scr, scope_scr, qg, dg, gq_acc,
):
    blocks = tokens // BLK
    width = BLK
    wide = group * BLK
    cut = next(c for c in (10, 5, 4, 2, 1) if slots % c == 0)
    chunk = cut * BLK
    scale = 1.0 / math.sqrt(width)
    log2e = scale * math.log2(math.e)

    def fill(d, _):
        tile = kv_ref[pl.ds(pl.multiple_of(d * (tokens + PAD) + tokens, PAD), PAD), 0:tokens]
        for b in range(blocks):
            row = tile[0:1, b * BLK : (b + 1) * BLK].astype(F32)
            at = pl.multiple_of((d * blocks + b) * BLK, BLK)
            scope_scr[pl.ds(at, BLK), :] = jnp.broadcast_to(row, (BLK, BLK)).T
        return 0

    lax.fori_loop(0, devices, fill, 0)

    def rows_of(j):
        d = j // blocks
        return pl.ds(pl.multiple_of(d * (tokens + PAD) + (j - d * blocks) * BLK, PAD), BLK)

    def head_loop(g, _):
        k_cols = pl.ds(pl.multiple_of(g * width, width), width)
        v_cols = pl.ds(pl.multiple_of((kv + g) * width, width), width)
        acc[...] = jnp.zeros_like(acc)

        def row_loop(r, _):
            q_rows = pl.ds(pl.multiple_of(r * BLK, BLK), BLK)

            def head_cols(n):
                return pl.ds(pl.multiple_of((g * group + n) * width, width), width)

            for n in range(group):
                qg[n * BLK : (n + 1) * BLK, :] = q_ref[q_rows, head_cols(n)]
                dg[n * BLK : (n + 1) * BLK, :] = do_ref[q_rows, head_cols(n)]
            own = own_ref[pl.ds(r, 1), :]

            def listed_rows(c):
                return [listed[r, c * cut + u] for u in range(cut)]

            def near(c, cols):
                return jnp.concatenate([kv_ref[rows_of(j), cols] for j in listed_rows(c)], axis=0)

            def here(c):
                return pl.ds(pl.multiple_of(c * chunk, chunk), chunk)

            def first(c, high):
                s = lax.dot_general(near(c, k_cols), qg[...], NT, preferred_element_type=F32)
                bias = []
                for j in listed_rows(c):
                    sk = scope_scr[pl.ds(pl.multiple_of(j * BLK, BLK), BLK), :]
                    b = jnp.where((sk == own) | (sk == 0.0), 0.0, -1e30)
                    bias.append(jnp.concatenate([b] * group, axis=1))
                s = s + jnp.concatenate(bias, axis=0)
                s_scr[here(c), :] = s
                return jnp.maximum(high, jnp.max(s, axis=0, keepdims=True))

            high = lax.fori_loop(0, slots // cut, first, jnp.full((1, wide), -1e30, F32))

            def second(c, carry):
                total, delta = carry
                p = jnp.exp2((s_scr[here(c), :] - high) * log2e)
                dp = lax.dot_general(near(c, v_cols), dg[...], NT, preferred_element_type=F32)
                s_scr[here(c), :] = p
                dp_scr[here(c), :] = dp
                return (
                    total + jnp.sum(p, axis=0, keepdims=True),
                    delta + jnp.sum(p * dp, axis=0, keepdims=True),
                )

            zero = jnp.zeros((1, wide), F32)
            total, delta = lax.fori_loop(0, slots // cut, second, (zero, zero))
            inverse = 1.0 / total
            delta = delta * inverse
            gq_acc[...] = jnp.zeros_like(gq_acc)

            def third(c, _):
                pn = s_scr[here(c), :] * inverse
                ds = (pn * ((dp_scr[here(c), :] - delta) * scale)).astype(BF16)
                gv = jnp.dot(pn.astype(BF16), dg[...], preferred_element_type=F32)
                gk = jnp.dot(ds, qg[...], preferred_element_type=F32)
                gq_acc[...] += lax.dot_general(near(c, k_cols), ds, TN, preferred_element_type=F32)
                for u, j in enumerate(listed_rows(c)):
                    at = pl.ds(pl.multiple_of(j * BLK, BLK), BLK)
                    acc[at, 0:width] += gk[u * BLK : (u + 1) * BLK, :]
                    acc[at, width : 2 * width] += gv[u * BLK : (u + 1) * BLK, :]
                return 0

            lax.fori_loop(0, slots // cut, third, 0)
            for n in range(group):
                gq_ref[q_rows, head_cols(n)] = gq_acc[:, n * BLK : (n + 1) * BLK].T.astype(BF16)
            return 0

        lax.fori_loop(0, blocks, row_loop, 0)
        part_ref[:, k_cols] = acc[:, 0:width].astype(BF16)
        part_ref[:, v_cols] = acc[:, width : 2 * width].astype(BF16)
        return 0

    lax.fori_loop(0, kv, head_loop, 0)


def attend(listed, q, do, kv_all, own, devices, kv):
    tokens = q.shape[0]
    group = q.shape[1] // BLK // kv
    slots = listed.shape[1]
    total = devices * tokens
    wide = group * BLK
    vmem = pl.BlockSpec(memory_space=pltpu.VMEM)
    return pl.pallas_call(
        functools.partial(attend_kernel, devices, tokens, kv, group, slots),
        out_shape=(
            jax.ShapeDtypeStruct(q.shape, BF16),
            jax.ShapeDtypeStruct((total, 2 * kv * BLK), BF16),
        ),
        in_specs=[pl.BlockSpec(memory_space=pltpu.SMEM)] + [vmem] * 4,
        out_specs=(vmem, vmem),
        scratch_shapes=[
            pltpu.VMEM((total, 2 * BLK), F32),
            pltpu.VMEM((slots * BLK, wide), F32),
            pltpu.VMEM((slots * BLK, wide), F32),
            pltpu.VMEM((total, BLK), F32),
            pltpu.VMEM((wide, BLK), BF16),
            pltpu.VMEM((wide, BLK), BF16),
            pltpu.VMEM((BLK, wide), F32),
        ],
        compiler_params=pltpu.CompilerParams(vmem_limit_bytes=56 * 2**20),
        name="attend",
    )(listed, q, do, kv_all, own)


def place(devices):
    me = lax.axis_index("ctx")
    a, b, c = me // 4, lax.rem(me // 2, 2), lax.rem(me, 2)
    return a, b, c, devices // 4


def greet(ctx_peers, head_peers):
    barrier = pltpu.get_barrier_semaphore()
    for peer in ctx_peers:
        pl.semaphore_signal(barrier, inc=1, device_id={"ctx": peer}, device_id_type=MESH)
    for peer in head_peers:
        pl.semaphore_signal(barrier, inc=1, device_id={"head": peer}, device_id_type=MESH)
    pl.semaphore_wait(barrier, len(ctx_peers) + len(head_peers))


def near_first(count):
    return sorted(range(1, count), key=lambda o: min(o, count - o))


def gather_kernel(
    devices, heads, block_ref, mixed_ref, weight_ref, all_ref, do_ref, wide, weight,
    z_send, z_recv, x_send, x_recv, c_send, c_recv, h_send, h_recv, own_sem,
):
    rows = block_ref.shape[0]
    width = mixed_ref.shape[1]
    a, b, c, count = place(devices)
    head = lax.axis_index("head")
    x_peer = a * 4 + (1 - b) * 2 + c
    c_peer = a * 4 + b * 2 + (1 - c)
    h_peers = {o: lax.rem(head + o, heads) for o in range(1, heads)}

    def slot(at, far, other):
        i = at * 4 + ((1 - b) if far else b) * 2 + ((1 - c) if other else c)
        return all_ref.at[pl.ds(pl.multiple_of(i * rows, PAD), rows)]

    def cols(h):
        return wide.at[:, pl.ds(pl.multiple_of(h * width, BLK), width)]

    barrier = pltpu.get_barrier_semaphore()
    for way in (1, -1):

        @pl.when((a + way >= 0) & (a + way < count))
        def _():
            pl.semaphore_signal(
                barrier, inc=1, device_id={"ctx": (a + way) * 4 + b * 2 + c}, device_id_type=MESH
            )

    for peer in (x_peer, c_peer):
        pl.semaphore_signal(barrier, inc=1, device_id={"ctx": peer}, device_id_type=MESH)
    for peer in h_peers.values():
        pl.semaphore_signal(barrier, inc=1, device_id={"head": peer}, device_id_type=MESH)
    inner = jnp.where((a > 0) & (a < count - 1), 1, 0)
    pl.semaphore_wait(barrier, 3 + len(h_peers) + inner)

    def copy(src, dst, send, recv, where):
        return pltpu.make_async_remote_copy(
            src_ref=src, dst_ref=dst, send_sem=send, recv_sem=recv,
            device_id=where, device_id_type=MESH,
        )

    def along(src, at, way, s):
        n = (0 if way > 0 else count) + s
        peer = (a + way) * 4 + b * 2 + c
        return copy(src, slot(at, False, False), z_send.at[n], z_recv.at[n], {"ctx": peer})

    def across(src, at):
        return copy(src, slot(at, False, False), x_send.at[at], x_recv.at[at], {"ctx": x_peer})

    def core(src, at, far):
        n = 2 * at + int(far)
        return copy(src, slot(at, far, False), c_send.at[n], c_recv.at[n], {"ctx": c_peer})

    def valid(at):
        return (at >= 0) & (at < count)

    load = pltpu.make_async_copy(weight_ref, weight, own_sem.at[2])
    load.start()
    keep = pltpu.make_async_copy(block_ref, slot(a, False, False), own_sem.at[0])
    keep.start()
    keep_mixed = pltpu.make_async_copy(mixed_ref, cols(head), own_sem.at[1])
    keep_mixed.start()
    across(block_ref, a).start()
    for way in (1, -1):

        @pl.when(valid(a + way))
        def _():
            along(block_ref, a, way, 0).start()

    to_head = {
        o: copy(mixed_ref, cols(head), h_send.at[o], h_recv.at[o], {"head": h_peers[o]})
        for o in h_peers
    }
    for out in to_head.values():
        out.start()
    core(block_ref, a, False).start()

    def over_x(at):
        got = slot(at, True, False)
        copy(got, got, x_send.at[at], x_recv.at[at], {"ctx": x_peer}).wait_recv()
        core(got, at, True).start()

    def over_x_of(s):
        for way in (1, -1):

            @pl.when(valid(a - way * s))
            def _():
                over_x(a - way * s)

    tile = 2 * BLK if weight.shape[0] % (2 * BLK) == 0 else BLK
    tiles = weight.shape[0] // tile
    edges = [tiles * t // (count - 1) for t in range(count)]

    def project(t, _):
        at = pl.multiple_of(t * tile, tile)
        made = lax.dot_general(
            wide[...], weight[pl.ds(at, tile), :], NT, preferred_element_type=F32
        )
        do_ref[:, pl.ds(at, tile)] = made.astype(BF16)
        return 0

    for s in range(1, count):
        for way in (1, -1):
            at = a - way * s

            @pl.when(valid(at))
            def _():
                got = slot(at, False, False)
                n = (0 if way > 0 else count) + s - 1
                peer = {"ctx": (a - way) * 4 + b * 2 + c}
                copy(got, got, z_send.at[n], z_recv.at[n], peer).wait_recv()

                @pl.when(valid(a + way))
                def _():
                    along(got, at, way, s).start()

                across(got, at).start()
                core(got, at, False).start()

        if s == 1:
            over_x(a)
        else:
            over_x_of(s - 1)
        if s == min(2, count - 1):
            keep_mixed.wait()
            load.wait()
            for o in h_peers:
                to = cols(lax.rem(head - o + heads, heads))
                copy(to, to, h_send.at[o], h_recv.at[o], {"head": h_peers[o]}).wait_recv()
            lax.fori_loop(0, edges[s], project, 0)
        elif s > 2:
            lax.fori_loop(edges[s - 1], edges[s], project, 0)
    over_x_of(count - 1)
    for at in range(count):
        for far in (False, True):
            n = 2 * at + int(far)
            got = slot(at, far, True)
            copy(got, got, c_send.at[n], c_recv.at[n], {"ctx": c_peer}).wait_recv()
    keep.wait()
    for out in to_head.values():
        out.wait_send()
    for way in (1, -1):
        for s in range(count - 1):

            @pl.when(valid(a - way * s) & valid(a + way))
            def _():
                at = a - way * s
                along(slot(at, False, False), at, way, s).wait_send()

    for at in range(count):
        across(slot(at, False, False), at).wait_send()
        for far in (False, True):
            core(slot(at, far, False), at, far).wait_send()


def gather(block, d_mixed, weight, devices, heads):
    count = devices // 4
    dma = pltpu.SemaphoreType.DMA
    hbm = pl.BlockSpec(memory_space=pl.ANY)
    tokens = d_mixed.shape[0]
    return pl.pallas_call(
        functools.partial(gather_kernel, devices, heads),
        out_shape=(
            jax.ShapeDtypeStruct((devices * block.shape[0], block.shape[1]), BF16),
            jax.ShapeDtypeStruct((tokens, weight.shape[0]), BF16),
        ),
        in_specs=[hbm, hbm, hbm],
        out_specs=(hbm, pl.BlockSpec(memory_space=pltpu.VMEM)),
        scratch_shapes=[
            pltpu.VMEM((tokens, heads * d_mixed.shape[1]), BF16),
            pltpu.VMEM(weight.shape, BF16),
            dma((2 * count,)), dma((2 * count,)), dma((count,)), dma((count,)),
            dma((2 * count,)), dma((2 * count,)), dma((heads,)), dma((heads,)), dma((3,)),
        ],
        compiler_params=pltpu.CompilerParams(
            collective_id=0, has_side_effects=True, vmem_limit_bytes=48 * 2**20
        ),
        name="gather",
    )(block, d_mixed, weight)


def scatter_kernel(
    devices, part_ref, home_ref, c_land, x_land, z_land, x_out, z_out,
    c_send, c_recv, x_send, x_recv, z_send, z_recv,
):
    rows = home_ref.shape[0]
    step = 32
    a, b, c, count = place(devices)
    order = near_first(count)[::-1] + [0]

    def part_at(o, far, other):
        i = lax.rem(a + o, count) * 4 + ((1 - b) if far else b) * 2 + ((1 - c) if other else c)
        return pl.multiple_of(i * rows, rows)

    z_peers = {o: lax.rem(a + o, count) * 4 + b * 2 + c for o in range(1, count)}
    x_peer = a * 4 + (1 - b) * 2 + c
    c_peer = a * 4 + b * 2 + (1 - c)
    greet(list(z_peers.values()) + [x_peer, c_peer], [])

    def copy(src, dst, send, recv, peer):
        return pltpu.make_async_remote_copy(
            src_ref=src, dst_ref=dst, send_sem=send, recv_sem=recv,
            device_id={"ctx": peer}, device_id_type=MESH,
        )

    core, across, along = {}, {}, {}
    for far in (True, False):
        for o in order:
            at = 2 * o + int(far)
            core[at] = copy(
                part_ref.at[pl.ds(part_at(o, far, True), rows)], c_land.at[at],
                c_send.at[at], c_recv.at[at], c_peer,
            )
            core[at].start()

    def add(out, at, terms):
        def body(i, _):
            here = pl.multiple_of(i * step, step)
            total = part_ref[pl.ds(at + here, step), :].astype(F32)
            for land, index in terms:
                total = total + land[index, pl.ds(here, step), :].astype(F32)
            out[pl.ds(here, step), :] = total.astype(BF16)
            return 0

        lax.fori_loop(0, rows // step, body, 0)

    for o in order:
        at = 2 * o + 1
        core[at].wait_recv()
        add(x_out.at[o], part_at(o, True, False), [(c_land, at)])
        across[o] = copy(x_out.at[o], x_land.at[o], x_send.at[o], x_recv.at[o], x_peer)
        across[o].start()
    for o in order:
        core[2 * o].wait_recv()
        across[o].wait_recv()
        terms = [(c_land, 2 * o), (x_land, o)]
        if o > 0:
            add(z_out.at[o], part_at(o, False, False), terms)
            along[o] = copy(z_out.at[o], z_land.at[o], z_send.at[o], z_recv.at[o], z_peers[o])
            along[o].start()
    for o in order[:-1]:
        along[o].wait_recv()
    add(
        home_ref,
        part_at(0, False, False),
        [(c_land, 0), (x_land, 0)] + [(z_land, o) for o in range(1, count)],
    )
    for made in (core, across, along):
        for out in made.values():
            out.wait_send()


def scatter(part, devices):
    count = devices // 4
    dma = pltpu.SemaphoreType.DMA
    vmem = pl.BlockSpec(memory_space=pltpu.VMEM)
    block = (part.shape[0] // devices, part.shape[1])
    return pl.pallas_call(
        functools.partial(scatter_kernel, devices),
        out_shape=jax.ShapeDtypeStruct(block, BF16),
        in_specs=[vmem],
        out_specs=vmem,
        scratch_shapes=[
            pltpu.VMEM((2 * count,) + block, BF16),
            pltpu.VMEM((count,) + block, BF16),
            pltpu.VMEM((count,) + block, BF16),
            pltpu.VMEM((count,) + block, BF16),
            pltpu.VMEM((count,) + block, BF16),
            dma((2 * count,)), dma((2 * count,)),
            dma((count,)), dma((count,)), dma((count,)), dma((count,)),
        ],
        compiler_params=pltpu.CompilerParams(
            collective_id=1, has_side_effects=True, vmem_limit_bytes=40 * 2**20
        ),
        name="scatter",
    )(part)


def on_device(devices, split, query, key, value, d_mixed, out_weight, block_keys, scope_ids):
    tokens, heads, width = query.shape
    kv = key.shape[1]
    cols = 2 * kv * width
    scope_rows = jnp.zeros((PAD, cols), BF16).at[:, :tokens].set(scope_ids.astype(BF16)[None, :])
    block = jnp.concatenate(
        [
            jnp.concatenate([key.reshape(tokens, -1), value.reshape(tokens, -1)], axis=1),
            scope_rows,
        ],
        axis=0,
    )
    kv_all, d_out = gather(block, d_mixed, out_weight, devices, split)
    own = scope_ids.astype(F32).reshape(tokens // BLK, BLK)
    grad_q, part = attend(
        block_keys, query.reshape(tokens, -1), d_out, kv_all, own, devices, kv
    )
    home = scatter(part, devices)
    half = kv * width
    return (
        grad_q.reshape(query.shape),
        home[:, :half].reshape(key.shape),
        home[:, half:].reshape(value.shape),
    )


def solution(mesh):
    in_specs = (
        P("ctx", "head", None),
        P("ctx", "head", None),
        P("ctx", "head", None),
        P("ctx", "head"),
        P("head", None),
        P("ctx", None),
        P("ctx"),
    )
    out_specs = (P("ctx", "head", None), P("ctx", "head", None), P("ctx", "head", None))
    return jax.shard_map(
        functools.partial(on_device, mesh.shape["ctx"], mesh.shape["head"]),
        mesh=mesh,
        in_specs=in_specs,
        out_specs=out_specs,
        check_vma=False,
    )
```
